256 devices in a mesh: grp: 16 (over x, y), ep: 16 (over z, core).
Axes of the slice: x: 4, y: 4, z: 8, core: 2. Of those that a mesh axis runs over, the one named last changes fastest.
Arguments:
- tokens: bfloat16 [16384, 1440], P(('grp', 'ep')), parts along dimension 0, may hold values from -6 to 6
- expert_ids: int32 [16384, 4], P(('grp', 'ep')), parts along dimension 0, may hold values from 0 to 15, as said below
- gate_weights: float32 [16384, 4], P(('grp', 'ep')), parts along dimension 0, may hold values from 0.1 to 1
- row_counts: int32 [256], P(('grp', 'ep')), parts along dimension 0, may hold values from 32 to 64, as said below
- w_gate: bfloat16 [16, 1440, 1440], P('ep'), may hold values from -0.15625 to 0.15625
- w_up: bfloat16 [16, 1440, 1440], P('ep'), may hold values from -0.15625 to 0.15625
- w_down: bfloat16 [16, 1440, 1440], P('ep'), may hold values from -0.15625 to 0.15625
Outputs:
- moe_out: bfloat16 [16384, 1440], P(('grp', 'ep')), parts along dimension 0
The draws below stay inside these ranges and needn't reach their ends.
There are 16 independent parts, one for each index of `grp`. The reference program is written for one: setup_inputs(seed, part) draws one part's arguments, and reference() takes and returns one part's arrays. A program takes and returns all parts, laid end to end along the dimension named above; an argument that names none is the same for every part. Nothing has to cross between parts.
Inputs may be any that keep to these rules, and one draw needn't show every extreme that they name: `expert_ids`: each row names 4 different experts; in the 64 rows of one device one expert, the hot one, the same on every device of a group, is named exactly 48 times, and every other expert at most 14 times, some exactly 14 times. `row_counts`: live rows are the first ones of a device's block; some device of each group has all 64 live.
All inputs are finite; a program needn't handle non-finite values.
Results may differ from the reference program's by a relative error of at most 0.0058.
Values may be sent and summed in bfloat16 or wider, within the bound.
No kernel may reach another device: no remote copies, remote signals or barrier semaphores. Data moves between devices by JAX's collectives and lax.ppermute only.
A program may use at most 128 MiB of HBM per device.

```python
import jax
import jax.numpy as jnp
from jax import lax

D = 1440
FF = 1440
TOP = 4
ROWS_DEV = 64
EXPERTS = 16
ROWS = 1024
CAP = 48


def draw_expert_ids(key, part):
    key = jax.random.fold_in(key, 11)
    hot_expert = jax.random.randint(jax.random.fold_in(key, 1), (), 0, EXPERTS)
    block_count = ROWS // ROWS_DEV
    others_count = EXPERTS - 1

    def one_block(block_index):
        block_key = jax.random.fold_in(key, block_index + 100)
        row_rank = jax.random.permutation(jax.random.fold_in(block_key, 1), ROWS_DEV).astype(jnp.int32)
        other_order = jax.random.permutation(jax.random.fold_in(block_key, 2), others_count).astype(jnp.int32)
        offset = jax.random.randint(jax.random.fold_in(block_key, 3), (), 0, others_count)
        columns = jnp.arange(TOP, dtype=jnp.int32)
        is_hot_row = row_rank[:, None] < CAP
        hot_spot = row_rank[:, None] * (TOP - 1) + columns[None, :] - 1
        cold_spot = CAP * (TOP - 1) + (row_rank[:, None] - CAP) * TOP + columns[None, :]
        spots = (offset + jnp.where(is_hot_row, hot_spot, cold_spot)) % others_count
        chosen = (hot_expert + 1 + other_order[spots]) % EXPERTS
        values = jnp.where(is_hot_row & (columns[None, :] == 0), hot_expert, chosen)
        turn = jax.random.randint(jax.random.fold_in(block_key, 4), (ROWS_DEV,), 0, TOP)
        order_index = (columns[None, :] + turn[:, None]) % TOP
        return jnp.take_along_axis(values, order_index, axis=1)
    blocks = jax.vmap(one_block)(jnp.arange(block_count, dtype=jnp.int32))
    return blocks.reshape(ROWS, TOP).astype(jnp.int32)


def draw_row_counts(key, part):
    key = jax.random.fold_in(key, 12)
    block_count = ROWS // ROWS_DEV
    counts = jax.random.randint(jax.random.fold_in(key, 1), (block_count,), ROWS_DEV // 2, ROWS_DEV + 1)
    full_block = jax.random.randint(jax.random.fold_in(key, 2), (), 0, block_count)
    positions = jnp.arange(block_count, dtype=jnp.int32)
    return jnp.where(positions == full_block, ROWS_DEV, counts).astype(jnp.int32)


def block_levels(stream_key, extent, split, least, high):
    def one(position, blocks):
        steps = jax.random.uniform(jax.random.fold_in(jax.random.fold_in(stream_key, 6), position), (blocks,), jnp.float32, least / len(split), high / len(split))
        return jnp.repeat(jnp.exp(steps), extent[position] // blocks).reshape((-1,) + (1,) * (len(extent) - position - 1))

    factor_of = one(*split[0])
    for cut in split[1:]:
        factor_of = factor_of * one(*cut)
    return factor_of


def gaussian(own_key, shape, scale, limit, pieces=(), kind=jnp.bfloat16):
    drawn = scale * jax.random.normal(own_key, shape, jnp.float32)
    if pieces:
        drawn = drawn * block_levels(own_key, shape, pieces, -0.22, 0.18)
    return jnp.clip(drawn, -limit, limit).astype(kind)


def setup_inputs(seed: int = 0, part: int = 0) -> dict:
    keys = jax.random.split(jax.random.key(seed), 8)
    part_splits = jax.random.split(jax.random.fold_in(keys[7], part), 8)
    tokens = gaussian(part_splits[0], (ROWS, D), 1.0, 6.0, ((0, 16),))
    expert_ids = draw_expert_ids(jax.random.fold_in(jax.random.fold_in(keys[7], part), 71), part)
    gate_weights = jnp.clip(0.1 + 0.9 * jax.random.uniform(part_splits[2], (ROWS, TOP), jnp.float32) ** block_levels(part_splits[2], (ROWS, TOP), ((0, 16),), -0.2, 0.2), 0.1, 1.0)
    row_counts = draw_row_counts(jax.random.fold_in(jax.random.fold_in(keys[7], part), 71), part)
    w_gate = gaussian(keys[4], (EXPERTS, D, FF), D ** -0.5, 0.15625, ((0, 16),))
    w_up = gaussian(keys[5], (EXPERTS, D, FF), D ** -0.5, 0.15625, ((0, 16),))
    w_down = gaussian(keys[6], (EXPERTS, FF, D), FF ** -0.5, 0.15625, ((0, 16),))
    return dict(tokens=tokens, expert_ids=expert_ids, gate_weights=gate_weights, row_counts=row_counts, w_gate=w_gate, w_up=w_up, w_down=w_down)


def expert_apply(row_block, gate_matrix, up_matrix, down_matrix):
    gate = jnp.dot(row_block, gate_matrix, preferred_element_type=jnp.float32)
    up_value = jnp.dot(row_block, up_matrix, preferred_element_type=jnp.float32)
    hidden = ((up_value + 1.0) * gate * jax.nn.sigmoid(1.702 * gate)).astype(jnp.bfloat16)
    return jnp.dot(hidden, down_matrix, preferred_element_type=jnp.float32).astype(jnp.bfloat16)


def reference(tokens, expert_ids, gate_weights, row_counts, w_gate, w_up, w_down):
    row_total = tokens.shape[0]
    index = jnp.arange(row_total, dtype=jnp.int32)
    live_rows = (index % ROWS_DEV) < row_counts[index // ROWS_DEV]
    flat_ids = expert_ids.reshape(-1)
    flat_live = jnp.repeat(live_rows, TOP)
    flat_weight = jnp.where(live_rows[:, None], gate_weights, 0.0).reshape(-1)
    flat_rows = jnp.arange(row_total * TOP, dtype=jnp.int32) // TOP
    most_rows = EXPERTS * CAP

    def scan_expert(combined, packed):
        expert_index, gate_matrix, up_matrix, down_matrix = packed
        match_pairs = (flat_ids == expert_index) & flat_live
        picked = jnp.nonzero(match_pairs, size=most_rows, fill_value=0)[0].astype(jnp.int32)
        valid = jnp.arange(most_rows, dtype=jnp.int32) < jnp.sum(match_pairs.astype(jnp.int32))
        source_rows = flat_rows[picked]
        outputs = expert_apply(tokens[source_rows], gate_matrix, up_matrix, down_matrix)
        scale = jnp.where(valid, flat_weight[picked], 0.0)
        return combined.at[source_rows].add(outputs.astype(jnp.float32) * scale[:, None]), None

    start = jnp.zeros((row_total, D), jnp.float32)
    combined, _ = lax.scan(scan_expert, start, (jnp.arange(EXPERTS, dtype=jnp.int32), w_gate, w_up, w_down))
    return combined.astype(jnp.bfloat16)
```

```python
import jax
import jax.numpy as jnp
from jax import lax
from jax.experimental import pallas as pl
from jax.experimental.pallas import tpu as pltpu
from jax.sharding import PartitionSpec as P

LANES = 128
BF16, F32 = jnp.bfloat16, jnp.float32


def pad_up(n, m):
    return -(-n // m) * m


def ring_pairs(n):
    chips = n // 2

    def odd(chip):
        return (chip - 1) % chips if chip % 2 == 0 else (chip + 1) % chips

    swap = [(i, i ^ 1) for i in range(n)]
    even_pairs = [(i, i ^ 2) for i in range(n)]
    odd_pairs = [(i, odd(i // 2) * 2 + i % 2) for i in range(n)]
    return swap, even_pairs, odd_pairs


def route_kernel(experts, count_ref, x_ref, ids_ref, gw_ref, out_ref):
    rows, width = x_ref.shape
    last = width // LANES * LANES
    start = width - last
    lane = lax.broadcasted_iota(jnp.int32, (rows, LANES), 1) - start
    expert = lane & (experts - 1)
    weight = jnp.zeros((rows, LANES), F32)
    ids, gw = ids_ref[...], gw_ref[...]
    for k in range(ids.shape[1]):
        weight += jnp.where(ids[:, k : k + 1] == expert, gw[:, k : k + 1], 0.0)
    live = lax.broadcasted_iota(jnp.int32, (rows, LANES), 0) < count_ref[0]
    weight = jnp.where(live, weight, 0.0)
    high = weight.astype(BF16).astype(F32)
    middle = (weight - high).astype(BF16).astype(F32)
    low = weight - high - middle
    part = jnp.where(lane < experts, high, jnp.where(lane < 2 * experts, middle, low))
    part = jnp.where((lane >= 0) & (lane < 3 * experts), part, 0.0)
    out_ref[:, :last] = x_ref[:, :last]
    tail = jnp.concatenate([x_ref[:, last:].astype(F32), jnp.zeros((rows, LANES - start), F32)], axis=1)
    out_ref[:, last:] = jnp.where(lane < 0, tail, part).astype(BF16)


def expert_kernel(experts, count, *refs):
    xs, (wg, wu, wd), ys, hidden = refs[:count], refs[count : count + 3], refs[count + 3 : -1], refs[-1]
    width, ff = wg.shape
    last = width // LANES * LANES
    start = width - last
    x = jnp.concatenate([r[:, :width] for r in xs], axis=0) if count > 1 else xs[0][:, :width]
    tail = jnp.concatenate([r[:, last : last + LANES] for r in xs], axis=0).astype(F32)
    lane = lax.broadcasted_iota(jnp.int32, tail.shape, 1) - start
    mine = (lane >= 0) & (lane < 3 * experts) & ((lane & (experts - 1)) == lax.axis_index("ep"))
    weight = jnp.sum(jnp.where(mine, tail, 0.0), axis=1, keepdims=True)
    for lo in range(0, ff, 256):
        hi = min(lo + 256, ff)
        gate = jnp.dot(x, wg[:, lo:hi], preferred_element_type=F32)
        up = jnp.dot(x, wu[:, lo:hi], preferred_element_type=F32)
        hidden[:, lo:hi] = ((up + 1.0) * gate * jax.nn.sigmoid(1.702 * gate)).astype(BF16)
    h = hidden[...]
    for lo in range(0, width, 256):
        hi = min(lo + 256, width)
        y = jnp.dot(h, wd[:, lo:hi], preferred_element_type=F32).astype(BF16).astype(F32)
        y = (y * weight).astype(BF16)
        at = 0
        for r in ys:
            r[:, lo:hi] = y[at : at + r.shape[0]]
            at += r.shape[0]


def experts_apply(experts, blocks, weights):
    width, ff = weights[0].shape
    total = sum(b.shape[0] for b in blocks)
    vmem = pl.BlockSpec(memory_space=pltpu.VMEM)
    return pl.pallas_call(
        lambda *refs: expert_kernel(experts, len(blocks), *refs),
        out_shape=[jax.ShapeDtypeStruct((b.shape[0], width), BF16) for b in blocks],
        in_specs=[vmem] * (len(blocks) + 3),
        out_specs=[vmem] * len(blocks),
        scratch_shapes=[pltpu.VMEM((total, ff), BF16)],
        compiler_params=pltpu.CompilerParams(vmem_limit_bytes=40 << 20),
        cost_estimate=pl.CostEstimate(flops=6 * total * width * ff, bytes_accessed=total * width * 4, transcendentals=total * ff),
        name="experts",
    )(*[pltpu.with_memory_space_constraint(b, pltpu.VMEM) for b in blocks], *weights)


def add(*terms):
    total = terms[0].astype(F32)
    for t in terms[1:]:
        total = total + t.astype(F32)
    return total.astype(BF16)


def local(tokens, expert_ids, gate_weights, row_counts, w_gate, w_up, w_down):
    n = lax.axis_size("ep")
    rows, width = tokens.shape
    half = rows // 2
    experts = n * w_gate.shape[0]
    swap, even, odd = ring_pairs(n)

    def send(x, pairs):
        return lax.ppermute(x, "ep", pairs)

    vmem = pl.BlockSpec(memory_space=pltpu.VMEM)
    weights = [pltpu.with_memory_space_constraint(w.reshape(w.shape[1:]), pltpu.VMEM) for w in (w_gate, w_up, w_down)]
    own = pl.pallas_call(
        lambda *refs: route_kernel(experts, *refs),
        out_shape=jax.ShapeDtypeStruct((rows, pad_up(width, LANES)), BF16),
        in_specs=[pl.BlockSpec(memory_space=pltpu.SMEM), vmem, vmem, vmem],
        out_specs=vmem,
        name="route",
    )(row_counts, tokens, expert_ids, gate_weights)

    def chip_sum(blocks):
        theirs = [send(b, swap) for b in blocks]
        out = experts_apply(experts, blocks + theirs, weights)
        k = len(blocks)
        return [add(out[i], send(out[k + i], swap)) for i in range(k)]

    e1, o1 = send(own, even), send(own, odd)
    (t0,) = chip_sum([own])
    e2, o2 = send(o1, even), send(e1, odd)
    te1, to1 = chip_sum([e1, o1])
    e3, o3 = send(o2, even), send(e2, odd)
    te2, to2 = chip_sum([e2, o2])
    e4, o4 = send(o3[:half], even), send(e3[half:], odd)
    te3, to3 = chip_sum([e3, o3])
    te4, to4 = chip_sum([e4, o4])
    re, ro = send(te4, even), send(to4, odd)
    ao3 = jnp.concatenate([add(to3[:half], re), to3[half:]], axis=0)
    ae3 = jnp.concatenate([te3[:half], add(te3[half:], ro)], axis=0)
    re, ro = send(ae3, even), send(ao3, odd)
    ao2, ae2 = add(to2, re), add(te2, ro)
    re, ro = send(ae2, even), send(ao2, odd)
    ao1, ae1 = add(to1, re), add(te1, ro)
    re, ro = send(ae1, even), send(ao1, odd)
    return add(t0, re, ro)


def solution(mesh):
    rows = P(("grp", "ep"), None)
    in_specs = (rows, rows, rows, P(("grp", "ep"))) + (P("ep", None, None),) * 3
    return jax.shard_map(local, mesh=mesh, in_specs=in_specs, out_specs=rows, check_vma=False)
```

```python
import jax
import jax.numpy as jnp
from jax import lax
from jax.experimental import pallas as pl
from jax.experimental.pallas import tpu as pltpu
from jax.sharding import PartitionSpec as P

LANES = 128
BF16, F32 = jnp.bfloat16, jnp.float32


def pad_up(n, m):
    return -(-n // m) * m


def ring_pairs(n):
    chips = n // 2

    def odd(chip):
        return (chip - 1) % chips if chip % 2 == 0 else (chip + 1) % chips

    swap = [(i, i ^ 1) for i in range(n)]
    even_pairs = [(i, i ^ 2) for i in range(n)]
    odd_pairs = [(i, odd(i // 2) * 2 + i % 2) for i in range(n)]
    return swap, even_pairs, odd_pairs


def route_kernel(experts, count_ref, x_ref, ids_ref, gw_ref, out_ref):
    rows, width = x_ref.shape
    last = width // LANES * LANES
    start = width - last
    column = lax.broadcasted_iota(jnp.int32, (LANES, rows), 0) - start
    expert = column & (experts - 1)
    weight = jnp.zeros((LANES, rows), F32)
    for k in range(ids_ref.shape[0]):
        weight += jnp.where(ids_ref[k : k + 1, :] == expert, gw_ref[k : k + 1, :], 0.0)
    live = lax.broadcasted_iota(jnp.int32, (LANES, rows), 1) < count_ref[0]
    weight = jnp.where(live, weight, 0.0)
    high = weight.astype(BF16).astype(F32)
    middle = (weight - high).astype(BF16).astype(F32)
    low = weight - high - middle
    part = jnp.where(column < experts, high, jnp.where(column < 2 * experts, middle, low))
    part = jnp.where((column >= 0) & (column < 3 * experts), part, 0.0).T
    out_ref[:, :last] = x_ref[:, :last]
    tail = jnp.concatenate([x_ref[:, last:].astype(F32), jnp.zeros((rows, LANES - start), F32)], axis=1)
    lane = lax.broadcasted_iota(jnp.int32, (rows, LANES), 1)
    out_ref[:, last:] = jnp.where(lane < start, tail, part).astype(BF16)


def expert_body(experts, xs, wg, wu, wd, ys, hidden, ready=lambda k: None):
    width, ff = wg.shape
    last = width // LANES * LANES
    start = width - last
    x = jnp.concatenate([r[:, :width] for r in xs], axis=0)
    tail = jnp.concatenate([r[:, last : last + LANES] for r in xs], axis=0).astype(F32)
    lane = lax.broadcasted_iota(jnp.int32, tail.shape, 1) - start
    mine = (lane >= 0) & (lane < 3 * experts) & ((lane & (experts - 1)) == lax.axis_index("ep"))
    weight = jnp.sum(jnp.where(mine, tail, 0.0), axis=1, keepdims=True)
    ready(0)
    for lo in range(0, ff, 256):
        hi = min(lo + 256, ff)
        gate = jnp.dot(x, wg[:, lo:hi], preferred_element_type=F32)
        up = jnp.dot(x, wu[:, lo:hi], preferred_element_type=F32)
        hidden[:, lo:hi] = ((up + 1.0) * gate * jax.nn.sigmoid(1.702 * gate)).astype(BF16)
    ready(1)
    h = hidden[...]
    for lo in range(0, width, 256):
        hi = min(lo + 256, width)
        y = jnp.dot(h, wd[:, lo:hi], preferred_element_type=F32).astype(BF16).astype(F32)
        y = (y * weight).astype(BF16)
        at = 0
        for r in ys:
            r[:, lo:hi] = y[at : at + r.shape[0]]
            at += r.shape[0]


def expert_kernel(experts, count, *refs):
    xs, (wg, wu, wd), ys, hidden = refs[:count], refs[count : count + 3], refs[count + 3 : -1], refs[-1]
    expert_body(experts, xs, wg, wu, wd, ys, hidden)


def first_kernel(experts, count, *refs):
    xs, far, ys = refs[:count], refs[count : count + 3], refs[count + 3 : 2 * count + 3]
    near, hidden, sems = refs[2 * count + 3 : 2 * count + 6], refs[-2], refs[-1]
    copies = [pltpu.make_async_copy(f.at[0], w, sems.at[k]) for k, (f, w) in enumerate(zip(far, near))]
    for c in copies:
        c.start()

    def ready(stage):
        for c in copies[:2] if stage == 0 else copies[2:]:
            c.wait()

    expert_body(experts, xs, *near, ys, hidden, ready)


def experts_apply(experts, blocks, weights):
    first = weights[0].ndim == 3
    width, ff = weights[0].shape[-2:]
    total, count = sum(b.shape[0] for b in blocks), len(blocks)
    vmem = pl.BlockSpec(memory_space=pltpu.VMEM)
    out_shape = [pltpu.VMEM((b.shape[0], width), BF16) for b in blocks]
    scratch = [pltpu.VMEM((total, ff), BF16)]
    if first:
        out_shape += [pltpu.VMEM(w.shape[1:], BF16) for w in weights]
        scratch += [pltpu.SemaphoreType.DMA((3,))]
        weights = [pltpu.with_memory_space_constraint(w, pltpu.HBM) for w in weights]
    else:
        weights = [pltpu.with_memory_space_constraint(w, pltpu.VMEM) for w in weights]
    kernel = first_kernel if first else expert_kernel
    out = pl.pallas_call(
        lambda *refs: kernel(experts, count, *refs),
        out_shape=out_shape,
        in_specs=[vmem] * count + [pl.BlockSpec(memory_space=pltpu.HBM if first else pltpu.VMEM)] * 3,
        out_specs=[vmem] * len(out_shape),
        scratch_shapes=scratch,
        compiler_params=pltpu.CompilerParams(vmem_limit_bytes=16 << 20),
        cost_estimate=pl.CostEstimate(flops=6 * total * width * ff, bytes_accessed=total * width * 4, transcendentals=total * ff),
        name="experts",
    )(*[pltpu.with_memory_space_constraint(b, pltpu.VMEM) for b in blocks], *weights)
    return (out[:count], out[count:]) if first else (out, None)


def add(*terms):
    total = terms[0].astype(F32)
    for t in terms[1:]:
        total = total + t.astype(F32)
    return total.astype(BF16)


def local(tokens, expert_ids, gate_weights, row_counts, w_gate, w_up, w_down):
    n = lax.axis_size("ep")
    rows, width = tokens.shape
    half = rows // 2
    experts = n * w_gate.shape[0]
    swap, even, odd = ring_pairs(n)

    def send(x, pairs):
        return lax.ppermute(x, "ep", pairs)

    def swapped(blocks):
        return [send(b, swap) for b in blocks]

    def chip_sum(out):
        k = len(out) // 2
        return [add(mine, theirs) for mine, theirs in zip(out[:k], swapped(out[k:]))]

    vmem = pl.BlockSpec(memory_space=pltpu.VMEM)
    own = pl.pallas_call(
        lambda *refs: route_kernel(experts, *refs),
        out_shape=pltpu.VMEM((rows, pad_up(width, LANES)), BF16),
        in_specs=[pl.BlockSpec(memory_space=pltpu.SMEM), vmem, vmem, vmem],
        out_specs=vmem,
        name="route",
    )(row_counts, tokens, expert_ids.T, gate_weights.T)

    e, o = send(own, even), send(own, odd)
    out, weights = experts_apply(experts, [own] + swapped([own]), [w_gate, w_up, w_down])
    sums = []
    for step in range(3):
        e, o, out = lax.optimization_barrier((e, o, out))
        if step < 2:
            next_e, next_o = send(o, even), send(e, odd)
        else:
            next_e, next_o = send(o[:half], even), send(e[half:], odd)
        sums.append(chip_sum(out))
        out, _ = experts_apply(experts, [e, o] + swapped([e, o]), weights)
        e, o = next_e, next_o
    e, o, out = lax.optimization_barrier((e, o, out))
    sums.append(chip_sum(out))
    out, _ = experts_apply(experts, [e, o] + swapped([e, o]), weights)
    (t0,), (te1, to1), (te2, to2), (te3, to3) = sums
    te4, to4 = chip_sum(out)
    te4, to4 = lax.optimization_barrier((te4, to4))
    re, ro = send(te4, even), send(to4, odd)
    ao3 = jnp.concatenate([add(to3[:half], re), to3[half:]], axis=0)
    ae3 = jnp.concatenate([te3[:half], add(te3[half:], ro)], axis=0)
    ae3, ao3 = lax.optimization_barrier((ae3, ao3))
    re, ro = send(ae3, even), send(ao3, odd)
    ao2, ae2 = lax.optimization_barrier((add(to2, re), add(te2, ro)))
    re, ro = send(ae2, even), send(ao2, odd)
    ao1, ae1 = lax.optimization_barrier((add(to1, re), add(te1, ro)))
    re, ro = send(ae1, even), send(ao1, odd)
    return add(t0, re, ro)


def solution(mesh):
    rows = P(("grp", "ep"), None)
    in_specs = (rows, rows, rows, P(("grp", "ep"))) + (P("ep", None, None),) * 3
    return jax.shard_map(local, mesh=mesh, in_specs=in_specs, out_specs=rows, check_vma=False)
```

```python
import jax
import jax.numpy as jnp
from jax import lax
from jax.experimental import pallas as pl
from jax.experimental.pallas import tpu as pltpu
from jax.sharding import PartitionSpec as P

LANES = 128
LOAD_COLUMNS = 512
LEAST_ROWS = 128
BF16, F32 = jnp.bfloat16, jnp.float32


def pad_up(n, m):
    return -(-n // m) * m


def ring_pairs(n):
    chips = n // 2

    def odd(chip):
        return (chip - 1) % chips if chip % 2 == 0 else (chip + 1) % chips

    swap = [(i, i ^ 1) for i in range(n)]
    even_pairs = [(i, i ^ 2) for i in range(n)]
    odd_pairs = [(i, odd(i // 2) * 2 + i % 2) for i in range(n)]
    across = [(i, (i + n // 2) % n) for i in range(n)]
    return swap, even_pairs, odd_pairs, across


def route_kernel(experts, count_ref, x_ref, ids_ref, gw_ref, out_ref):
    rows, width = x_ref.shape
    last = width // LANES * LANES
    start = width - last
    column = lax.broadcasted_iota(jnp.int32, (LANES, rows), 0) - start
    expert = column & (experts - 1)
    weight = jnp.zeros((LANES, rows), F32)
    for k in range(ids_ref.shape[0]):
        weight += jnp.where(ids_ref[k : k + 1, :] == expert, gw_ref[k : k + 1, :], 0.0)
    live = lax.broadcasted_iota(jnp.int32, (LANES, rows), 1) < count_ref[0]
    weight = jnp.where(live, weight, 0.0)
    high = weight.astype(BF16).astype(F32)
    middle = (weight - high).astype(BF16).astype(F32)
    low = weight - high - middle
    part = jnp.where(column < experts, high, jnp.where(column < 2 * experts, middle, low))
    part = jnp.where((column >= 0) & (column < 3 * experts), part, 0.0).T
    out_ref[:, :last] = x_ref[:, :last]
    tail = jnp.concatenate([x_ref[:, last:].astype(F32), jnp.zeros((rows, LANES - start), F32)], axis=1)
    lane = lax.broadcasted_iota(jnp.int32, (rows, LANES), 1)
    out_ref[:, last:] = jnp.where(lane < start, tail, part).astype(BF16)


def expert_body(experts, xs, parts, hidden, ready, partials, ys):
    width, ff = parts[0][1].shape
    last = width // LANES * LANES
    start = width - last
    x = jnp.concatenate([r[:, :width] for r in xs], axis=0)
    filler = LEAST_ROWS - x.shape[0]
    if filler > 0:
        x = jnp.concatenate([x, jnp.zeros((filler, width), x.dtype)], axis=0)
    tail = jnp.concatenate([r[:, last : last + LANES] for r in xs], axis=0).astype(F32)
    lane = lax.broadcasted_iota(jnp.int32, tail.shape, 1) - start
    rows = x.shape[0]
    weight = []
    for k, (who, wg, wu, _) in enumerate(parts):
        mine = (lane >= 0) & (lane < 3 * experts) & ((lane & (experts - 1)) == who)
        weight.append(jnp.sum(jnp.where(mine, tail, 0.0), axis=1, keepdims=True))
        for lo in range(0, ff, 256):
            hi = min(lo + 256, ff)
            ready(k, lo, (0, 1))
            gate = jnp.dot(x, wg[:, lo:hi], preferred_element_type=F32)
            up = jnp.dot(x, wu[:, lo:hi], preferred_element_type=F32)
            hidden[k * rows : (k + 1) * rows, lo:hi] = ((up + 1.0) * gate * jax.nn.sigmoid(1.702 * gate)).astype(BF16)
    for lo in range(0, width, 256):
        hi = min(lo + 256, width)
        total = jnp.concatenate([r[:, lo:hi] for r in partials], axis=0) if partials else 0.0
        for k, (_, _, _, wd) in enumerate(parts):
            ready(k, lo, (2,))
            y = jnp.dot(hidden[k * rows : (k + 1) * rows, :], wd[:, lo:hi], preferred_element_type=F32)
            total = total + y[: tail.shape[0]].astype(BF16).astype(F32) * weight[k]
        at = 0
        for r in ys:
            r[:, lo:hi] = total[at : at + r.shape[0]].astype(r.dtype)
            at += r.shape[0]


def experts_apply(experts, blocks, near, far, partials, cut, dtype, fetch=()):
    sets = [w for w in (near, far) if w is not None]
    load = sets[0][0].ndim == 3
    width, ff = sets[0][0].shape[-2:]
    total, count = sum(b.shape[0] for b in blocks), len(blocks)
    vmem = pl.BlockSpec(memory_space=pltpu.VMEM)
    hbm = pl.BlockSpec(memory_space=pltpu.HBM)
    pieces = total // cut
    held = [*(sets[0] if load else ()), *fetch]
    out_shape = [pltpu.VMEM((cut, width), dtype)] * pieces + [pltpu.VMEM(w.shape[1:], BF16) for w in held]
    rows = max(total, LEAST_ROWS)
    scratch = [pltpu.VMEM((rows * len(sets), ff), BF16)]
    cuts = list(range(0, ff, LOAD_COLUMNS))
    if held:
        scratch += [pltpu.SemaphoreType.DMA((len(held), len(cuts)))]

    def body(*refs):
        refs = list(refs)

        def take(k):
            out = refs[:k]
            del refs[:k]
            return out

        xs, ps = take(count), take(len(partials))
        weights = [take(3) for _ in sets]
        sources = [*(weights[0] if load else ()), *take(len(fetch))]
        ys, targets = take(pieces), take(len(held))
        copies = {}
        for j, (source, target) in enumerate(zip(sources, targets)):
            for c, lo in enumerate(cuts):
                part = pl.ds(lo, min(LOAD_COLUMNS, ff - lo))
                copies[j, lo] = pltpu.make_async_copy(source.at[0, :, part], target.at[:, part], refs[-1].at[j, c])
        for j, lo in sorted(copies, key=lambda key: (key[0] // 2, key[1])):
            copies[j, lo].start()
        waited = set()

        def ready(k, lo, which):
            for j in which:
                if load and k == 0 and (j, lo) in copies:
                    copies[j, lo].wait()
                    waited.add((j, lo))

        if load:
            weights[0] = targets[:3]
        me = lax.axis_index("ep")
        who = ([me] if near is not None else []) + ([me ^ 1] if far is not None else [])
        expert_body(experts, xs, [(i, *w) for i, w in zip(who, weights)], refs[0], ready, ps, ys)
        for key in copies:
            if key not in waited:
                copies[key].wait()

    def hold(arrays, space):
        return [pltpu.with_memory_space_constraint(a, space) for a in arrays]

    out = pl.pallas_call(
        body,
        out_shape=out_shape,
        in_specs=[vmem] * (count + len(partials))
        + [hbm if load else vmem] * 3
        + [vmem] * (3 * len(sets) - 3)
        + [hbm] * len(fetch),
        out_specs=[vmem] * len(out_shape),
        scratch_shapes=scratch,
        compiler_params=pltpu.CompilerParams(vmem_limit_bytes=12 << 20),
        cost_estimate=pl.CostEstimate(
            flops=6 * total * width * ff * len(sets), bytes_accessed=total * width * 4, transcendentals=total * ff
        ),
        name="experts",
    )(
        *hold([*blocks, *partials], pltpu.VMEM),
        *hold(sets[0], pltpu.HBM if load else pltpu.VMEM),
        *[a for w in sets[1:] for a in hold(w, pltpu.VMEM)],
        *hold(fetch, pltpu.HBM),
    )
    return (out[:pieces], out[pieces:]) if held else out


def add(*terms):
    total = terms[0].astype(F32)
    for t in terms[1:]:
        total = total + t.astype(F32)
    return total.astype(BF16)


def local(tokens, expert_ids, gate_weights, row_counts, w_gate, w_up, w_down):
    n = lax.axis_size("ep")
    rows, width = tokens.shape
    half = rows // 2
    experts = n * w_gate.shape[0]
    swap, even, odd, across = ring_pairs(n)

    def send(x, pairs):
        return lax.ppermute(x, "ep", pairs)

    vmem = pl.BlockSpec(memory_space=pltpu.VMEM)
    own = pl.pallas_call(
        lambda *refs: route_kernel(experts, *refs),
        out_shape=pltpu.VMEM((rows, pad_up(width, LANES)), BF16),
        in_specs=[pl.BlockSpec(memory_space=pltpu.SMEM), vmem, vmem, vmem],
        out_specs=vmem,
        compiler_params=pltpu.CompilerParams(vmem_limit_bytes=4 << 20),
        name="route",
    )(row_counts, *[pltpu.with_memory_space_constraint(x, pltpu.HBM) for x in (tokens, expert_ids.T, gate_weights.T)])

    fence = lax.optimization_barrier
    far = [send(w.reshape(w.shape[1:]), swap) for w in (w_gate, w_up, w_down)]

    e1, o1 = send(own, even), send(own, odd)
    p0, near = experts_apply(experts, [own], [w_gate, w_up, w_down], None, [], rows, F32)
    e1, o1, p0 = fence((e1, o1, p0))
    e2, o2 = send(o1, even), send(e1, odd)
    p1 = experts_apply(experts, [e1, o1], near, None, [], rows, F32)
    e2, o2, p1 = fence((e2, o2, p1))
    e3, o3 = send(o2, even), send(e2, odd)
    p2 = experts_apply(experts, [e2, o2], near, None, [], rows, F32)
    p2, p1, far = fence((p2, p1, far))
    t0, te1, to1 = experts_apply(experts, [own, e1, o1], None, far, [*p0, *p1], rows, BF16)
    e3, o3, p2, t0 = fence((e3, o3, p2, t0))
    e4, o4 = send(o3[:half], even), send(e3[half:], odd)
    te3, to3 = experts_apply(experts, [e3, o3], near, far, [], rows, BF16)
    te3, to3, e4, o4 = fence((te3, to3, e4, o4))
    re, ro = send(te3, even), send(to3, odd)
    (t4,) = experts_apply(experts, [e4, o4], near, far, [], rows, BF16)
    r4 = send(t4, across)
    te2, to2 = experts_apply(experts, [e2, o2], None, far, p2, rows, BF16)
    te2, to2, re, ro = fence((te2, to2, re, ro))
    re, ro = send(add(te2, ro), even), send(add(to2, re), odd)
    re, ro = send(add(te1, ro), even), send(add(to1, re), odd)
    return add(t0, r4, re, ro)


def solution(mesh):
    rows = P(("grp", "ep"), None)
    in_specs = (rows, rows, rows, P(("grp", "ep"))) + (P("ep", None, None),) * 3
    return jax.shard_map(local, mesh=mesh, in_specs=in_specs, out_specs=rows, check_vma=False)
```

```python
import jax
import jax.numpy as jnp
from jax import lax
from jax.experimental import pallas as pl
from jax.experimental.pallas import tpu as pltpu
from jax.sharding import PartitionSpec as P

LANES = 128
LOAD_COLUMNS = 512
LEAST_ROWS = 128
BF16, F32 = jnp.bfloat16, jnp.float32


def pad_up(n, m):
    return -(-n // m) * m


def ring_pairs(n):
    chips = n // 2

    def odd(chip):
        return (chip - 1) % chips if chip % 2 == 0 else (chip + 1) % chips

    swap = [(i, i ^ 1) for i in range(n)]
    even_pairs = [(i, i ^ 2) for i in range(n)]
    odd_pairs = [(i, odd(i // 2) * 2 + i % 2) for i in range(n)]
    across = [(i, (i + n // 2) % n) for i in range(n)]
    return swap, even_pairs, odd_pairs, across


def route_kernel(experts, count_ref, x_ref, ids_ref, gw_ref, out_ref):
    rows, width = x_ref.shape
    last = width // LANES * LANES
    start = width - last
    column = lax.broadcasted_iota(jnp.int32, (LANES, rows), 0) - start
    expert = column & (experts - 1)
    weight = jnp.zeros((LANES, rows), F32)
    for k in range(ids_ref.shape[0]):
        weight += jnp.where(ids_ref[k : k + 1, :] == expert, gw_ref[k : k + 1, :], 0.0)
    live = lax.broadcasted_iota(jnp.int32, (LANES, rows), 1) < count_ref[0]
    weight = jnp.where(live, weight, 0.0)
    high = weight.astype(BF16).astype(F32)
    middle = (weight - high).astype(BF16).astype(F32)
    low = weight - high - middle
    part = jnp.where(column < experts, high, jnp.where(column < 2 * experts, middle, low))
    part = jnp.where((column >= 0) & (column < 3 * experts), part, 0.0).T
    out_ref[:, :last] = x_ref[:, :last]
    tail = jnp.concatenate([x_ref[:, last:].astype(F32), jnp.zeros((rows, LANES - start), F32)], axis=1)
    lane = lax.broadcasted_iota(jnp.int32, (rows, LANES), 1)
    out_ref[:, last:] = jnp.where(lane < start, tail, part).astype(BF16)


def expert_body(experts, xs, parts, hidden, ready, partials, ys):
    width, ff = parts[0][1].shape
    last = width // LANES * LANES
    start = width - last
    x = jnp.concatenate([r[:, :width] for r in xs], axis=0)
    filler = LEAST_ROWS - x.shape[0]
    if filler > 0:
        x = jnp.concatenate([x, jnp.zeros((filler, width), x.dtype)], axis=0)
    tail = jnp.concatenate([r[:, last : last + LANES] for r in xs], axis=0).astype(F32)
    lane = lax.broadcasted_iota(jnp.int32, tail.shape, 1) - start
    rows = x.shape[0]
    weight = []
    for k, (who, wg, wu, _) in enumerate(parts):
        mine = (lane >= 0) & (lane < 3 * experts) & ((lane & (experts - 1)) == who)
        weight.append(jnp.sum(jnp.where(mine, tail, 0.0), axis=1, keepdims=True))
        for lo in range(0, ff, 256):
            hi = min(lo + 256, ff)
            ready(k, lo, (0, 1))
            gate = jnp.dot(x, wg[:, lo:hi], preferred_element_type=F32)
            up = jnp.dot(x, wu[:, lo:hi], preferred_element_type=F32)
            hidden[k * rows : (k + 1) * rows, lo:hi] = ((up + 1.0) * gate * jax.nn.sigmoid(1.702 * gate)).astype(BF16)
    for lo in range(0, width, 256):
        hi = min(lo + 256, width)
        total = jnp.concatenate([r[:, lo:hi] for r in partials], axis=0) if partials else 0.0
        for k, (_, _, _, wd) in enumerate(parts):
            ready(k, lo, (2,))
            y = jnp.dot(hidden[k * rows : (k + 1) * rows, :], wd[:, lo:hi], preferred_element_type=F32)
            total = total + y[: tail.shape[0]].astype(BF16).astype(F32) * weight[k]
        at = 0
        for r in ys:
            r[:, lo:hi] = total[at : at + r.shape[0]].astype(r.dtype)
            at += r.shape[0]


def experts_apply(experts, blocks, near, far, partials, cut, dtype, fetch=()):
    sets = [w for w in (near, far) if w is not None]
    load = sets[0][0].ndim == 3
    width, ff = sets[0][0].shape[-2:]
    total, count = sum(b.shape[0] for b in blocks), len(blocks)
    vmem = pl.BlockSpec(memory_space=pltpu.VMEM)
    hbm = pl.BlockSpec(memory_space=pltpu.HBM)
    pieces = total // cut
    held = [*(sets[0] if load else ()), *fetch]
    out_shape = [pltpu.VMEM((cut, width), dtype)] * pieces + [pltpu.VMEM(w.shape[1:], BF16) for w in held]
    rows = max(total, LEAST_ROWS)
    scratch = [pltpu.VMEM((rows * len(sets), ff), BF16)]
    cuts = list(range(0, ff, LOAD_COLUMNS))
    if held:
        scratch += [pltpu.SemaphoreType.DMA((len(held), len(cuts)))]

    def body(*refs):
        refs = list(refs)

        def take(k):
            out = refs[:k]
            del refs[:k]
            return out

        xs, ps = take(count), take(len(partials))
        weights = [take(3) for _ in sets]
        sources = [*(weights[0] if load else ()), *take(len(fetch))]
        ys, targets = take(pieces), take(len(held))
        copies = {}
        for j, (source, target) in enumerate(zip(sources, targets)):
            for c, lo in enumerate(cuts):
                part = pl.ds(lo, min(LOAD_COLUMNS, ff - lo))
                copies[j, lo] = pltpu.make_async_copy(source.at[0, :, part], target.at[:, part], refs[-1].at[j, c])
        for j, lo in sorted(copies, key=lambda key: (key[0] // 2, key[1])):
            copies[j, lo].start()
        waited = set()

        def ready(k, lo, which):
            for j in which:
                if load and k == 0 and (j, lo) in copies:
                    copies[j, lo].wait()
                    waited.add((j, lo))

        if load:
            weights[0] = targets[:3]
        me = lax.axis_index("ep")
        who = ([me] if near is not None else []) + ([me ^ 1] if far is not None else [])
        expert_body(experts, xs, [(i, *w) for i, w in zip(who, weights)], refs[0], ready, ps, ys)
        for key in copies:
            if key not in waited:
                copies[key].wait()

    def hold(arrays, space):
        return [pltpu.with_memory_space_constraint(a, space) for a in arrays]

    out = pl.pallas_call(
        body,
        out_shape=out_shape,
        in_specs=[vmem] * (count + len(partials))
        + [hbm if load else vmem] * 3
        + [vmem] * (3 * len(sets) - 3)
        + [hbm] * len(fetch),
        out_specs=[vmem] * len(out_shape),
        scratch_shapes=scratch,
        compiler_params=pltpu.CompilerParams(vmem_limit_bytes=12 << 20),
        cost_estimate=pl.CostEstimate(
            flops=6 * total * width * ff * len(sets), bytes_accessed=total * width * 4, transcendentals=total * ff
        ),
        name="experts",
    )(
        *hold([*blocks, *partials], pltpu.VMEM),
        *hold(sets[0], pltpu.HBM if load else pltpu.VMEM),
        *[a for w in sets[1:] for a in hold(w, pltpu.VMEM)],
        *hold(fetch, pltpu.HBM),
    )
    return (out[:pieces], out[pieces:]) if held else out


def add(*terms):
    total = terms[0].astype(F32)
    for t in terms[1:]:
        total = total + t.astype(F32)
    return total.astype(BF16)


def local(tokens, expert_ids, gate_weights, row_counts, w_gate, w_up, w_down):
    n = lax.axis_size("ep")
    rows, width = tokens.shape
    half = rows // 2
    experts = n * w_gate.shape[0]
    swap, even, odd, across = ring_pairs(n)

    def send(x, pairs):
        return lax.ppermute(x, "ep", pairs)

    vmem = pl.BlockSpec(memory_space=pltpu.VMEM)
    own = pl.pallas_call(
        lambda *refs: route_kernel(experts, *refs),
        out_shape=pltpu.VMEM((rows, pad_up(width, LANES)), BF16),
        in_specs=[pl.BlockSpec(memory_space=pltpu.SMEM), vmem, vmem, vmem],
        out_specs=vmem,
        compiler_params=pltpu.CompilerParams(vmem_limit_bytes=4 << 20),
        name="route",
    )(row_counts, *[pltpu.with_memory_space_constraint(x, pltpu.HBM) for x in (tokens, expert_ids.T, gate_weights.T)])

    fence = lax.optimization_barrier
    far = [send(w.reshape(w.shape[1:]), swap) for w in (w_gate, w_up, w_down)]

    e1, o1 = send(own, even), send(own, odd)
    p0, near = experts_apply(experts, [own], [w_gate, w_up, w_down], None, [], rows, F32)
    e1, o1, p0 = fence((e1, o1, p0))
    e2, o2 = send(o1, even), send(e1, odd)
    p1 = experts_apply(experts, [e1, o1], near, None, [], rows, F32)
    e2, o2, p1 = fence((e2, o2, p1))
    e3, o3 = send(o2, even), send(e2, odd)
    te2, to2 = experts_apply(experts, [e2, o2], near, far, [], rows, BF16)
    e3, o3, te2, to2 = fence((e3, o3, te2, to2))
    e4, o4 = send(o3[:half], even), send(e3[half:], odd)
    te3, to3 = experts_apply(experts, [e3, o3], near, far, [], rows, BF16)
    te3, to3, e4, o4 = fence((te3, to3, e4, o4))
    re, ro = send(te3, even), send(to3, odd)
    (t4,) = experts_apply(experts, [e4, o4], near, far, [], rows, BF16)
    te2, to2, t4, p0, p1 = fence((add(te2, ro), add(to2, re), t4, p0, p1))
    re, ro = send(te2, even), send(to2, odd)
    r4 = send(t4, across)
    t0, te1, to1 = experts_apply(experts, [own, e1, o1], None, far, [*p0, *p1], rows, BF16)
    te1, to1, t0 = fence((add(te1, ro), add(to1, re), t0))
    re, ro = send(te1, even), send(to1, odd)
    return add(t0, r4, re, ro)


def solution(mesh):
    rows = P(("grp", "ep"), None)
    in_specs = (rows, rows, rows, P(("grp", "ep"))) + (P("ep", None, None),) * 3
    return jax.shard_map(local, mesh=mesh, in_specs=in_specs, out_specs=rows, check_vma=False)
```

```python
import jax
import jax.numpy as jnp
from jax import lax
from jax.experimental import pallas as pl
from jax.experimental.pallas import tpu as pltpu
from jax.sharding import PartitionSpec as P

LANES = 128
LOAD_COLUMNS = 512
LEAST_ROWS = 128
BF16, F32 = jnp.bfloat16, jnp.float32


def pad_up(n, m):
    return -(-n // m) * m


def ring_pairs(n):
    chips = n // 2

    def odd(chip):
        return (chip - 1) % chips if chip % 2 == 0 else (chip + 1) % chips

    swap = [(i, i ^ 1) for i in range(n)]
    even_pairs = [(i, i ^ 2) for i in range(n)]
    odd_pairs = [(i, odd(i // 2) * 2 + i % 2) for i in range(n)]
    across = [(i, (i + n // 2) % n) for i in range(n)]
    return swap, even_pairs, odd_pairs, across


def route_kernel(experts, count_ref, x_ref, ids_ref, gw_ref, out_ref):
    rows, width = x_ref.shape
    last = width // LANES * LANES
    start = width - last
    column = lax.broadcasted_iota(jnp.int32, (LANES, rows), 0) - start
    expert = column & (experts - 1)
    weight = jnp.zeros((LANES, rows), F32)
    for k in range(ids_ref.shape[0]):
        weight += jnp.where(ids_ref[k : k + 1, :] == expert, gw_ref[k : k + 1, :], 0.0)
    live = lax.broadcasted_iota(jnp.int32, (LANES, rows), 1) < count_ref[0]
    weight = jnp.where(live, weight, 0.0)
    high = weight.astype(BF16).astype(F32)
    middle = (weight - high).astype(BF16).astype(F32)
    low = weight - high - middle
    part = jnp.where(column < experts, high, jnp.where(column < 2 * experts, middle, low))
    part = jnp.where((column >= 0) & (column < 3 * experts), part, 0.0).T
    out_ref[:, :last] = x_ref[:, :last]
    tail = jnp.concatenate([x_ref[:, last:].astype(F32), jnp.zeros((rows, LANES - start), F32)], axis=1)
    lane = lax.broadcasted_iota(jnp.int32, (rows, LANES), 1)
    out_ref[:, last:] = jnp.where(lane < start, tail, part).astype(BF16)


def expert_body(experts, xs, parts, hidden, ready, partials, ys):
    width, ff = parts[0][1].shape
    last = width // LANES * LANES
    start = width - last
    x = jnp.concatenate([r[:, :width] for r in xs], axis=0)
    filler = LEAST_ROWS - x.shape[0]
    if filler > 0:
        x = jnp.concatenate([x, jnp.zeros((filler, width), x.dtype)], axis=0)
    tail = jnp.concatenate([r[:, last : last + LANES] for r in xs], axis=0).astype(F32)
    lane = lax.broadcasted_iota(jnp.int32, tail.shape, 1) - start
    rows = x.shape[0]
    weight = []
    for k, (who, wg, wu, _) in enumerate(parts):
        mine = (lane >= 0) & (lane < 3 * experts) & ((lane & (experts - 1)) == who)
        weight.append(jnp.sum(jnp.where(mine, tail, 0.0), axis=1, keepdims=True))
        for lo in range(0, ff, 256):
            hi = min(lo + 256, ff)
            ready(k, lo, (0, 1))
            gate = jnp.dot(x, wg[:, lo:hi], preferred_element_type=F32)
            up = jnp.dot(x, wu[:, lo:hi], preferred_element_type=F32)
            hidden[k * rows : (k + 1) * rows, lo:hi] = ((up + 1.0) * gate * jax.nn.sigmoid(1.702 * gate)).astype(BF16)
    for lo in range(0, width, 256):
        hi = min(lo + 256, width)
        total = jnp.concatenate([r[:, lo:hi] for r in partials], axis=0) if partials else 0.0
        for k, (_, _, _, wd) in enumerate(parts):
            ready(k, lo, (2,))
            y = jnp.dot(hidden[k * rows : (k + 1) * rows, :], wd[:, lo:hi], preferred_element_type=F32)
            total = total + y[: tail.shape[0]].astype(BF16).astype(F32) * weight[k]
        at = 0
        for r in ys:
            r[:, lo:hi] = total[at : at + r.shape[0]].astype(r.dtype)
            at += r.shape[0]


def experts_apply(experts, blocks, near, far, partials, cut, dtype, fetch=()):
    sets = [w for w in (near, far) if w is not None]
    load = sets[0][0].ndim == 3
    width, ff = sets[0][0].shape[-2:]
    total, count = sum(b.shape[0] for b in blocks), len(blocks)
    vmem = pl.BlockSpec(memory_space=pltpu.VMEM)
    hbm = pl.BlockSpec(memory_space=pltpu.HBM)
    pieces = total // cut
    held = [*(sets[0] if load else ()), *fetch]
    out_shape = [pltpu.VMEM((cut, width), dtype)] * pieces + [pltpu.VMEM(w.shape[1:], BF16) for w in held]
    rows = max(total, LEAST_ROWS)
    scratch = [pltpu.VMEM((rows * len(sets), ff), BF16)]
    cuts = list(range(0, ff, LOAD_COLUMNS))
    if held:
        scratch += [pltpu.SemaphoreType.DMA((len(held), len(cuts)))]

    def body(*refs):
        refs = list(refs)

        def take(k):
            out = refs[:k]
            del refs[:k]
            return out

        xs, ps = take(count), take(len(partials))
        weights = [take(3) for _ in sets]
        sources = [*(weights[0] if load else ()), *take(len(fetch))]
        ys, targets = take(pieces), take(len(held))
        copies = {}
        for j, (source, target) in enumerate(zip(sources, targets)):
            for c, lo in enumerate(cuts):
                part = pl.ds(lo, min(LOAD_COLUMNS, ff - lo))
                copies[j, lo] = pltpu.make_async_copy(source.at[0, :, part], target.at[:, part], refs[-1].at[j, c])
        for j, lo in sorted(copies, key=lambda key: (key[0] // 2, key[1])):
            copies[j, lo].start()
        waited = set()

        def ready(k, lo, which):
            for j in which:
                if load and k == 0 and (j, lo) in copies:
                    copies[j, lo].wait()
                    waited.add((j, lo))

        if load:
            weights[0] = targets[:3]
        me = lax.axis_index("ep")
        who = ([me] if near is not None else []) + ([me ^ 1] if far is not None else [])
        expert_body(experts, xs, [(i, *w) for i, w in zip(who, weights)], refs[0], ready, ps, ys)
        for key in copies:
            if key not in waited:
                copies[key].wait()

    def hold(arrays, space):
        return [pltpu.with_memory_space_constraint(a, space) for a in arrays]

    out = pl.pallas_call(
        body,
        out_shape=out_shape,
        in_specs=[vmem] * (count + len(partials))
        + [hbm if load else vmem] * 3
        + [vmem] * (3 * len(sets) - 3)
        + [hbm] * len(fetch),
        out_specs=[vmem] * len(out_shape),
        scratch_shapes=scratch,
        compiler_params=pltpu.CompilerParams(vmem_limit_bytes=12 << 20),
        cost_estimate=pl.CostEstimate(
            flops=6 * total * width * ff * len(sets), bytes_accessed=total * width * 4, transcendentals=total * ff
        ),
        name="experts",
    )(
        *hold([*blocks, *partials], pltpu.VMEM),
        *hold(sets[0], pltpu.HBM if load else pltpu.VMEM),
        *[a for w in sets[1:] for a in hold(w, pltpu.VMEM)],
        *hold(fetch, pltpu.HBM),
    )
    return (out[:pieces], out[pieces:]) if held else out


def add(*terms):
    total = terms[0].astype(F32)
    for t in terms[1:]:
        total = total + t.astype(F32)
    return total.astype(BF16)


def local(tokens, expert_ids, gate_weights, row_counts, w_gate, w_up, w_down):
    n = lax.axis_size("ep")
    rows, width = tokens.shape
    half = rows // 2
    experts = n * w_gate.shape[0]
    swap, even, odd, across = ring_pairs(n)

    def send(x, pairs):
        return lax.ppermute(x, "ep", pairs)

    vmem = pl.BlockSpec(memory_space=pltpu.VMEM)
    own = pl.pallas_call(
        lambda *refs: route_kernel(experts, *refs),
        out_shape=pltpu.VMEM((rows, pad_up(width, LANES)), BF16),
        in_specs=[pl.BlockSpec(memory_space=pltpu.SMEM), vmem, vmem, vmem],
        out_specs=vmem,
        compiler_params=pltpu.CompilerParams(vmem_limit_bytes=4 << 20),
        name="route",
    )(row_counts, *[pltpu.with_memory_space_constraint(x, pltpu.HBM) for x in (tokens, expert_ids.T, gate_weights.T)])

    fence = lax.optimization_barrier
    far = [send(w.reshape(w.shape[1:]), swap) for w in (w_gate, w_up, w_down)]

    e1, o1 = send(own, even), send(own, odd)
    p0, near = experts_apply(experts, [own], [w_gate, w_up, w_down], None, [], rows, F32)
    e1, o1, p0 = fence((e1, o1, p0))
    e2, o2 = send(o1, even), send(e1, odd)
    p1 = experts_apply(experts, [e1, o1], near, None, [], rows, F32)
    e2, o2, p1 = fence((e2, o2, p1))
    e3, o3 = send(o2, even), send(e2, odd)
    te2, to2 = experts_apply(experts, [e2, o2], near, far, [], rows, BF16)
    e3, o3, te2, to2 = fence((e3, o3, te2, to2))
    d4 = send(o3, even)
    te3, to3 = experts_apply(experts, [e3, o3], near, far, [], rows, BF16)
    te3, to3, d4 = fence((te3, to3, d4))
    re, ro = send(te3, even), send(to3, odd)
    (t4,) = experts_apply(experts, [d4], near, far, [], rows, BF16)
    te2, to2, t4, p0, p1 = fence((add(te2, ro), add(to2, re), t4, p0, p1))
    re, ro = send(te2, even), send(to2, odd)
    r4 = send(t4, across)
    t0, te1, to1 = experts_apply(experts, [own, e1, o1], None, far, [*p0, *p1], rows, BF16)
    te1, to1, t0 = fence((add(te1, ro), add(to1, re), t0))
    re, ro = send(te1, even), send(to1, odd)
    return add(t0, r4, re, ro)


def solution(mesh):
    rows = P(("grp", "ep"), None)
    in_specs = (rows, rows, rows, P(("grp", "ep"))) + (P("ep", None, None),) * 3
    return jax.shard_map(local, mesh=mesh, in_specs=in_specs, out_specs=rows, check_vma=False)
```

```python
import jax
import jax.numpy as jnp
from jax import lax
from jax.experimental import pallas as pl
from jax.experimental.pallas import tpu as pltpu
from jax.sharding import PartitionSpec as P

LANES = 128
LOAD_COLUMNS = 512
LEAST_ROWS = 128
BF16, F32 = jnp.bfloat16, jnp.float32


def pad_up(n, m):
    return -(-n // m) * m


def ring_pairs(n):
    chips = n // 2

    def odd(chip):
        return (chip - 1) % chips if chip % 2 == 0 else (chip + 1) % chips

    swap = [(i, i ^ 1) for i in range(n)]
    even_pairs = [(i, i ^ 2) for i in range(n)]
    odd_pairs = [(i, odd(i // 2) * 2 + i % 2) for i in range(n)]
    across = [(i, (i + n // 2) % n) for i in range(n)]
    return swap, even_pairs, odd_pairs, across


def route_kernel(experts, count_ref, x_ref, ids_ref, gw_ref, out_ref):
    rows, width = x_ref.shape
    last = width // LANES * LANES
    start = width - last
    column = lax.broadcasted_iota(jnp.int32, (LANES, rows), 0) - start
    expert = column & (experts - 1)
    weight = jnp.zeros((LANES, rows), F32)
    for k in range(ids_ref.shape[0]):
        weight += jnp.where(ids_ref[k : k + 1, :] == expert, gw_ref[k : k + 1, :], 0.0)
    live = lax.broadcasted_iota(jnp.int32, (LANES, rows), 1) < count_ref[0]
    weight = jnp.where(live, weight, 0.0)
    high = weight.astype(BF16).astype(F32)
    middle = (weight - high).astype(BF16).astype(F32)
    low = weight - high - middle
    part = jnp.where(column < experts, high, jnp.where(column < 2 * experts, middle, low))
    part = jnp.where((column >= 0) & (column < 3 * experts), part, 0.0).T
    out_ref[:, :last] = x_ref[:, :last]
    tail = jnp.concatenate([x_ref[:, last:].astype(F32), jnp.zeros((rows, LANES - start), F32)], axis=1)
    lane = lax.broadcasted_iota(jnp.int32, (rows, LANES), 1)
    out_ref[:, last:] = jnp.where(lane < start, tail, part).astype(BF16)


def expert_body(experts, xs, parts, hidden, ready, partials, ys):
    width, ff = parts[0][1].shape
    last = width // LANES * LANES
    start = width - last
    x = jnp.concatenate([r[:, :width] for r in xs], axis=0)
    filler = LEAST_ROWS - x.shape[0]
    if filler > 0:
        x = jnp.concatenate([x, jnp.zeros((filler, width), x.dtype)], axis=0)
    tail = jnp.concatenate([r[:, last : last + LANES] for r in xs], axis=0).astype(F32)
    lane = lax.broadcasted_iota(jnp.int32, tail.shape, 1) - start
    rows = x.shape[0]
    weight = []
    for k, (who, wg, wu, _) in enumerate(parts):
        mine = (lane >= 0) & (lane < 3 * experts) & ((lane & (experts - 1)) == who)
        weight.append(jnp.sum(jnp.where(mine, tail, 0.0), axis=1, keepdims=True))
        for lo in range(0, ff, 256):
            hi = min(lo + 256, ff)
            ready(k, lo, (0, 1))
            gate = jnp.dot(x, wg[:, lo:hi], preferred_element_type=F32)
            up = jnp.dot(x, wu[:, lo:hi], preferred_element_type=F32)
            hidden[k * rows : (k + 1) * rows, lo:hi] = ((up + 1.0) * gate * jax.nn.sigmoid(1.702 * gate)).astype(BF16)
    for lo in range(0, width, 256):
        hi = min(lo + 256, width)
        total = jnp.concatenate([r[:, lo:hi] for r in partials], axis=0) if partials else 0.0
        for k, (_, _, _, wd) in enumerate(parts):
            ready(k, lo, (2,))
            y = jnp.dot(hidden[k * rows : (k + 1) * rows, :], wd[:, lo:hi], preferred_element_type=F32)
            total = total + y[: tail.shape[0]].astype(BF16).astype(F32) * weight[k]
        at = 0
        for r in ys:
            r[:, lo:hi] = total[at : at + r.shape[0]].astype(r.dtype)
            at += r.shape[0]


def experts_apply(experts, blocks, near, far, partials, cut, dtype, fetch=()):
    sets = [w for w in (near, far) if w is not None]
    load = sets[0][0].ndim == 3
    width, ff = sets[0][0].shape[-2:]
    total, count = sum(b.shape[0] for b in blocks), len(blocks)
    vmem = pl.BlockSpec(memory_space=pltpu.VMEM)
    hbm = pl.BlockSpec(memory_space=pltpu.HBM)
    pieces = total // cut
    held = [*(sets[0] if load else ()), *fetch]
    out_shape = [pltpu.VMEM((cut, width), dtype)] * pieces + [pltpu.VMEM(w.shape[1:], BF16) for w in held]
    rows = max(total, LEAST_ROWS)
    scratch = [pltpu.VMEM((rows * len(sets), ff), BF16)]
    cuts = list(range(0, ff, LOAD_COLUMNS))
    if held:
        scratch += [pltpu.SemaphoreType.DMA((len(held), len(cuts)))]

    def body(*refs):
        refs = list(refs)

        def take(k):
            out = refs[:k]
            del refs[:k]
            return out

        xs, ps = take(count), take(len(partials))
        weights = [take(3) for _ in sets]
        sources = [*(weights[0] if load else ()), *take(len(fetch))]
        ys, targets = take(pieces), take(len(held))
        copies = {}
        for j, (source, target) in enumerate(zip(sources, targets)):
            for c, lo in enumerate(cuts):
                part = pl.ds(lo, min(LOAD_COLUMNS, ff - lo))
                copies[j, lo] = pltpu.make_async_copy(source.at[0, :, part], target.at[:, part], refs[-1].at[j, c])
        for j, lo in sorted(copies, key=lambda key: (key[0] // 2, key[1])):
            copies[j, lo].start()
        waited = set()

        def ready(k, lo, which):
            for j in which:
                if load and k == 0 and (j, lo) in copies:
                    copies[j, lo].wait()
                    waited.add((j, lo))

        if load:
            weights[0] = targets[:3]
        me = lax.axis_index("ep")
        who = ([me] if near is not None else []) + ([me ^ 1] if far is not None else [])
        expert_body(experts, xs, [(i, *w) for i, w in zip(who, weights)], refs[0], ready, ps, ys)
        for key in copies:
            if key not in waited:
                copies[key].wait()

    def hold(arrays, space):
        return [pltpu.with_memory_space_constraint(a, space) for a in arrays]

    out = pl.pallas_call(
        body,
        out_shape=out_shape,
        in_specs=[vmem] * (count + len(partials))
        + [hbm if load else vmem] * 3
        + [vmem] * (3 * len(sets) - 3)
        + [hbm] * len(fetch),
        out_specs=[vmem] * len(out_shape),
        scratch_shapes=scratch,
        compiler_params=pltpu.CompilerParams(vmem_limit_bytes=12 << 20),
        cost_estimate=pl.CostEstimate(
            flops=6 * total * width * ff * len(sets), bytes_accessed=total * width * 4, transcendentals=total * ff
        ),
        name="experts",
    )(
        *hold([*blocks, *partials], pltpu.VMEM),
        *hold(sets[0], pltpu.HBM if load else pltpu.VMEM),
        *[a for w in sets[1:] for a in hold(w, pltpu.VMEM)],
        *hold(fetch, pltpu.HBM),
    )
    return (out[:pieces], out[pieces:]) if held else out


def add(*terms):
    total = terms[0].astype(F32)
    for t in terms[1:]:
        total = total + t.astype(F32)
    return total.astype(BF16)


def local(tokens, expert_ids, gate_weights, row_counts, w_gate, w_up, w_down):
    n = lax.axis_size("ep")
    rows, width = tokens.shape
    half = rows // 2
    experts = n * w_gate.shape[0]
    swap, even, odd, across = ring_pairs(n)

    def send(x, pairs):
        return lax.ppermute(x, "ep", pairs)

    vmem = pl.BlockSpec(memory_space=pltpu.VMEM)
    own = pl.pallas_call(
        lambda *refs: route_kernel(experts, *refs),
        out_shape=pltpu.VMEM((rows, pad_up(width, LANES)), BF16),
        in_specs=[pl.BlockSpec(memory_space=pltpu.SMEM), vmem, vmem, vmem],
        out_specs=vmem,
        compiler_params=pltpu.CompilerParams(vmem_limit_bytes=4 << 20),
        name="route",
    )(row_counts, *[pltpu.with_memory_space_constraint(x, pltpu.HBM) for x in (tokens, expert_ids.T, gate_weights.T)])

    fence = lax.optimization_barrier
    far = [send(w.reshape(w.shape[1:]), swap) for w in (w_gate, w_up, w_down)]

    e1, o1 = send(own, even), send(own, odd)
    p0, near = experts_apply(experts, [own], [w_gate, w_up, w_down], None, [], rows, F32)
    e1, o1, p0 = fence((e1, o1, p0))
    e2, o2 = send(o1, even), send(e1, odd)
    p1 = experts_apply(experts, [e1, o1], near, None, [], rows, F32)
    e2, o2, p1 = fence((e2, o2, p1))
    e3, o3 = send(o2, even), send(e2, odd)
    te2, to2 = experts_apply(experts, [e2, o2], near, far, [], rows, BF16)
    e3, o3, te2, to2 = fence((e3, o3, te2, to2))
    d4 = send(o3, even)
    te3, to3 = experts_apply(experts, [e3, o3], near, far, [], rows, BF16)
    te3, to3, d4 = fence((te3, to3, d4))
    re, ro = send(te3, even), send(to3, odd)
    (t4,) = experts_apply(experts, [d4], near, far, [], rows, BF16)
    te2, to2, t4, p0, p1 = fence((add(te2, ro), add(to2, re), t4, p0, p1))
    re, ro = send(te2, even), send(to2, odd)
    r4 = send(t4, across)
    te1, to1 = experts_apply(experts, [e1, o1], None, far, p1, rows, BF16)
    te1, to1, p0 = fence((add(te1, ro), add(to1, re), p0))
    re, ro = send(te1, even), send(to1, odd)
    (t0,) = experts_apply(experts, [own], None, far, p0, rows, BF16)
    return add(t0, r4, re, ro)


def solution(mesh):
    rows = P(("grp", "ep"), None)
    in_specs = (rows, rows, rows, P(("grp", "ep"))) + (P("ep", None, None),) * 3
    return jax.shard_map(local, mesh=mesh, in_specs=in_specs, out_specs=rows, check_vma=False)
```
